256 devices in a mesh: dx: 32 (over y, z), dy: 8 (over x, core).
Axes of the slice: x: 4, y: 4, z: 8, core: 2. Of those that a mesh axis runs over, the one named last changes fastest.
Arguments:
- positions: float32 [32, 8, 3, 128], P('dx', 'dy'), may hold values from 0 to 1
- velocities: float32 [32, 8, 3, 128], P('dx', 'dy'), may hold values from -3 to 3
- species: int32 [32, 8, 128], P('dx', 'dy'), may hold values from 0 to 3
- neighbours: int32 [32, 8, 16, 128], P('dx', 'dy'), may hold values from -1 to 1151, as said below
- emb: bfloat16 [4, 28], replicated, may hold values from -4 to 4
- w_in: bfloat16 [128, 64], replicated, may hold values from -0.75 to 0.75
- w_two: bfloat16 [64, 128], replicated, may hold values from -0.5 to 0.5
- w_val: bfloat16 [192, 64], replicated, may hold values from -0.75 to 0.75
- w_env: bfloat16 [192, 64], replicated, may hold values from -0.75 to 0.75
- w_mix: bfloat16 [128, 256], replicated, may hold values from -0.375 to 0.375
- w_lat: bfloat16 [64, 128], replicated, may hold values from -0.5 to 0.5
- w_out: float32 [64], replicated, may hold values from -0.75 to 0.75
Outputs:
- positions_out: float32 [32, 8, 3, 128], P('dx', 'dy')
- velocities_out: float32 [32, 8, 3, 128], P('dx', 'dy')
- forces_out: float32 [32, 8, 3, 128], P('dx', 'dy')
The draws below stay inside these ranges and needn't reach their ends.
Inputs may be any that keep to these rules, and one draw needn't show every extreme that they name: `neighbours`: -1 marks an empty slot; every other entry is a ghost number o * 128 + a whose atom a lies in a block of domain slot o that has some entry of 0 or more, and never the slot's own centre. The blocks with any entry of 0 or more come first in each domain; every atom of such a block has at least 12 filled slots, placed first. Every domain has at least 4 such blocks and some domain has all 16.
All inputs are finite; a program needn't handle non-finite values.
Results may differ from the reference program's by a relative error of at most 0.04.
Values sent between devices are 32-bit elements; how exact they have to be, the bound alone decides.
A program may use at most 128 MiB of HBM per device.

```python
import math
import jax
import jax.numpy as jnp
from jax import lax

C = 64
HID = 128
EMB = 28
NBASIS = 8
NS = 4
SLOTS = 16
BLOCK = 128
STEPS = 2
ATOM_DEV = 128
CENTERS = 8
NB = 16
GROUP = 8
ZIN = 64
DOM_X = 32
DOM_Y = 8


def draw_neighbours(key, part):
    key = jax.random.fold_in(key, 7)
    key_r, key_o, key_a, key_c = jax.random.split(key, 4)
    rows = jnp.arange(DOM_X, dtype=jnp.int32)
    cols = jnp.arange(DOM_Y, dtype=jnp.int32)
    dist = jnp.abs(rows - DOM_X // 2)[:, None]
    jitter = jax.random.randint(key_r, (DOM_X, DOM_Y), 0, max(NB // 8, 1))
    live = jnp.maximum(NB - NB // 4 * dist - jitter * (dist > 0).astype(jnp.int32), NB // 4)
    alive = CENTERS * live
    shape = (DOM_X, DOM_Y, NB, BLOCK)
    slot_pick = jax.random.randint(key_o, shape, 0, 9)
    step_a = slot_pick // 3 - 1
    step_b = slot_pick % 3 - 1
    near_x = (rows[:, None, None, None] + step_a) % DOM_X
    near_y = (cols[None, :, None, None] + step_b) % DOM_Y
    near = alive[near_x, near_y]
    atom = jax.random.randint(key_a, shape, 0, 1 << 20) % near
    block_ids = jnp.arange(NB, dtype=jnp.int32)[None, None, :, None]
    edge_ids = jnp.arange(BLOCK, dtype=jnp.int32)[None, None, None, :]
    centre = block_ids * CENTERS + edge_ids // SLOTS
    atom = jnp.where((slot_pick == 4) & (atom == centre), (atom + 1) % near, atom)
    counts = jax.random.randint(key_c, (DOM_X, DOM_Y, NB, CENTERS), SLOTS - SLOTS // 4, SLOTS + 1)
    filled = edge_ids % SLOTS < jnp.repeat(counts, SLOTS, axis=3)
    used = filled & (block_ids < live[:, :, None, None])
    result = jnp.where(used, slot_pick * ATOM_DEV + atom, -1).astype(jnp.int32)
    return result.at[DOM_X // 2 - 1, 0, 0, 0].set(9 * ATOM_DEV - 1)


def set_ends(entries, key, low, top_value):
    shape = entries.shape
    spot = [jax.random.randint(jax.random.fold_in(key, axis), (), 0, shape[axis]) for axis in range(len(shape))]
    entries = entries.at[tuple(spot)].set(low)
    longest = shape.index(max(shape))
    spot[longest] = (spot[longest] + 1) % shape[longest]
    return entries.at[tuple(spot)].set(top_value)


def levels(stream_key, shape, shards, least, top_value):
    def one(axis_at, parts):
        heights = jax.random.uniform(jax.random.fold_in(jax.random.fold_in(stream_key, 6), axis_at), (parts,), jnp.float32, least / len(shards), top_value / len(shards))
        return jnp.repeat(jnp.exp(heights), shape[axis_at] // parts).reshape((-1,) + (1,) * (len(shape) - axis_at - 1))

    gain = one(*shards[0])
    for cut in shards[1:]:
        gain = gain * one(*cut)
    return gain


def bell_draw(stream_key, extent, scale, limit, pieces=(), kind=jnp.bfloat16):
    drawn = scale * jax.random.normal(stream_key, extent, jnp.float32)
    if pieces:
        drawn = drawn * levels(stream_key, extent, pieces, -0.22, 0.18)
    return jnp.clip(drawn, -limit, limit).astype(kind)


def setup_inputs(seed: int = 0) -> dict:
    keys = jax.random.split(jax.random.key(seed), 13)
    positions = jnp.clip(1.0 * jax.random.uniform(keys[0], (DOM_X, DOM_Y, 3, ATOM_DEV), jnp.float32) ** levels(keys[0], (DOM_X, DOM_Y, 3, ATOM_DEV), ((0, 32), (1, 8)), -0.2, 0.2), 0.0, 1.0)
    velocities = bell_draw(keys[1], (DOM_X, DOM_Y, 3, ATOM_DEV), 0.5, 3.0, ((0, 32), (1, 8)), jnp.float32)
    species = set_ends(jax.random.randint(keys[2], (DOM_X, DOM_Y, ATOM_DEV), 0, NS), jax.random.fold_in(keys[2], 1), 0, NS - 1).astype(jnp.int32)
    neighbours = draw_neighbours(jax.random.fold_in(keys[12], 71), 0)
    emb = bell_draw(keys[4], (NS, EMB), 1.0, 4.0)
    w_in = bell_draw(keys[5], (HID, ZIN), ZIN ** -0.5, 0.75)
    w_two = bell_draw(keys[6], (C, HID), HID ** -0.5, 0.5)
    w_val = bell_draw(keys[7], (3 * C, C), C ** -0.5, 0.75)
    w_env = bell_draw(keys[8], (3 * C, C), C ** -0.5, 0.75)
    w_mix = bell_draw(keys[9], (HID, 4 * C), (4 * C) ** -0.5, 0.375)
    w_lat = bell_draw(keys[10], (C, HID), HID ** -0.5, 0.5)
    w_out = bell_draw(keys[11], (C,), C ** -0.5, 0.75, (), jnp.float32)
    return {"positions": positions, "velocities": velocities, "species": species, "neighbours": neighbours, "emb": emb, "w_in": w_in, "w_two": w_two, "w_val": w_val, "w_env": w_env, "w_mix": w_mix, "w_lat": w_lat, "w_out": w_out}


TIME_STEP = 0.2
CUTOFF = 4.5
SOFTEN = 0.04
MASSES = (3.0, 2.0, 1.5, 1.0)

def matmul(left, right):
    return jnp.dot(left.astype(jnp.float32), right.astype(jnp.float32), preferred_element_type=jnp.float32)

def harmonics(unit):
    ux, uy, uz = (unit[0], unit[1], unit[2])
    root3 = math.sqrt(3.0)
    root5 = math.sqrt(5.0)
    root15 = math.sqrt(15.0)
    return jnp.stack([jnp.ones_like(ux), root3 * ux, root3 * uy, root3 * uz, root15 * ux * uy, root15 * uy * uz, 0.5 * root5 * (3.0 * uz * uz - 1.0), root15 * ux * uz, 0.5 * root15 * (ux * ux - uy * uy)])

def spread_orders(table):
    return jnp.concatenate([table[0:1], jnp.repeat(table[1:2], 3, axis=0), jnp.repeat(table[2:3], 5, axis=0)], axis=0)

def edge_energy(rel, valid, feats, params):
    w_in, w_two, w_val, w_env, w_mix, w_lat, w_out = params
    edges = rel.shape[1]
    dist_sq = lax.optimization_barrier(jnp.sum(rel * rel, axis=0)) + SOFTEN
    dist = jnp.sqrt(dist_sq)
    unit = rel / dist
    cut = valid * (1.0 - dist_sq / (CUTOFF * CUTOFF)) ** 2
    freq = jnp.arange(1, NBASIS + 1, dtype=jnp.float32)[:, None]
    basis = jnp.sin(freq * (math.pi / CUTOFF) * dist) / dist * cut
    sph = harmonics(unit)
    zin = jnp.concatenate([basis.astype(jnp.bfloat16), feats], axis=0)
    hidden = jax.nn.silu(matmul(w_in, zin)).astype(jnp.bfloat16)
    latent = matmul(w_two, hidden) * cut
    latent_b = latent.astype(jnp.bfloat16)
    value = matmul(w_val, latent_b).reshape(3, C, edges)
    envw = matmul(w_env, latent_b).reshape(3, C, edges)
    env = (spread_orders(envw) * sph[:, None, :]).reshape(9, C, edges // SLOTS, SLOTS).sum(axis=3) / SLOTS
    env_rep = jnp.repeat(env, SLOTS, axis=2)
    prod = spread_orders(value) * sph[:, None, :] * env_rep
    scal = jnp.concatenate([prod[0], prod[1:4].sum(axis=0), prod[4:9].sum(axis=0)], axis=0)
    mixed = jnp.concatenate([latent, scal], axis=0).astype(jnp.bfloat16)
    hidden2 = jax.nn.silu(matmul(w_mix, mixed)).astype(jnp.bfloat16)
    final = latent + matmul(w_lat, hidden2)
    return jnp.sum(w_out[:, None] * final * cut)

def group_grads(rel4, feats, params):
    nblk = rel4.shape[1]
    width = rel4.shape[2]
    rel = rel4[:3].reshape(3, nblk * width)
    valid = rel4[3].reshape(nblk * width)
    flat_feats = feats.reshape(feats.shape[0], nblk * width)

    def compute(unused):
        return jax.grad(edge_energy)(rel, valid, flat_feats, params).reshape(3, nblk, width)

    def skipped(unused):
        return jnp.zeros((3, nblk, width), jnp.float32)
    return lax.cond(jnp.any(valid > 0.0), compute, skipped, 0)

def species_lookup(emb, kinds):
    onehot = (kinds.reshape(-1)[None, :] == jnp.arange(NS, dtype=jnp.int32)[:, None]).astype(jnp.float32)
    looked = matmul(emb.T, onehot).astype(jnp.bfloat16)
    return looked.reshape((emb.shape[1],) + kinds.shape)

def build_edges(coords, ghost_kinds, place, kinds, nbrs, emb):
    nblk = nbrs.shape[0]
    valid = (nbrs >= 0).astype(jnp.float32)
    index = jnp.maximum(nbrs, 0)
    far_end = coords[:, index]
    centre = jnp.repeat(place.reshape(3, nblk, CENTERS), SLOTS, axis=2)
    rel4 = jnp.concatenate([far_end - centre, valid[None]], axis=0)
    centre_kind = jnp.repeat(kinds.reshape(nblk, CENTERS), SLOTS, axis=1)
    far_kind = ghost_kinds[index]
    feats = jnp.concatenate([species_lookup(emb, centre_kind), species_lookup(emb, far_kind)], axis=0)
    return (rel4, feats)

def split_terms(grads, nbrs, atoms):
    nblk = nbrs.shape[0]
    valid = (nbrs >= 0).astype(jnp.float32)
    masked = grads * valid[None]
    centre = masked.reshape(3, nblk, CENTERS, SLOTS).sum(axis=3).reshape(3, atoms)
    index = jnp.maximum(nbrs, 0).reshape(-1)
    ghost = jax.vmap(lambda comp: jax.ops.segment_sum(comp, index, num_segments=9 * atoms))(masked.reshape(3, -1))
    return (centre, -ghost)

def forces_all(place, kinds, nbrs, emb, params):
    dom_a, dom_b, three, atoms = place.shape
    nblk = nbrs.shape[2]
    ghosts = []
    ghost_kinds = []
    for pidx in range(3):
        for qidx in range(3):
            shift = jnp.array([pidx - 1, qidx - 1, 0], dtype=jnp.float32)[:, None]
            ghosts.append(jnp.roll(place, (1 - pidx, 1 - qidx), (0, 1)) + shift)
            ghost_kinds.append(jnp.roll(kinds, (1 - pidx, 1 - qidx), (0, 1)))
    coords = jnp.stack(ghosts, axis=3).reshape(dom_a * dom_b, 3, 9 * atoms)
    gkinds = jnp.stack(ghost_kinds, axis=2).reshape(dom_a * dom_b, 9 * atoms)
    devices = dom_a * dom_b
    rel4, feats = jax.vmap(build_edges, in_axes=(0, 0, 0, 0, 0, None))(coords, gkinds, place.reshape(devices, 3, atoms), kinds.reshape(devices, atoms), nbrs.reshape(devices, nblk, -1), emb)
    width = rel4.shape[3]
    groups = nblk // GROUP
    rel_g = rel4.reshape(devices, 4, groups, GROUP, width).transpose(0, 2, 1, 3, 4).reshape(devices * groups, 4, GROUP, width)
    feat_g = feats.reshape(devices, feats.shape[1], groups, GROUP, width).transpose(0, 2, 1, 3, 4).reshape(devices * groups, feats.shape[1], GROUP, width)
    grads = lax.map(lambda pair: group_grads(pair[0], pair[1], params), (rel_g, feat_g))
    grads = grads.reshape(devices, groups, 3, GROUP, width).transpose(0, 2, 1, 3, 4).reshape(devices, 3, nblk, width)
    centre, ghost = jax.vmap(split_terms, in_axes=(0, 0, None))(grads, nbrs.reshape(devices, nblk, -1), atoms)
    total = centre.reshape(dom_a, dom_b, 3, atoms)
    ghost = ghost.reshape(dom_a, dom_b, 3, 9, atoms)
    for pidx in range(3):
        for qidx in range(3):
            total = total + jnp.roll(ghost[:, :, :, 3 * pidx + qidx], (pidx - 1, qidx - 1), (0, 1))
    return total

def reference(positions, velocities, species, neighbours, emb, w_in, w_two, w_val, w_env, w_mix, w_lat, w_out):
    params = (w_in, w_two, w_val, w_env, w_mix, w_lat, w_out)
    mass = jnp.zeros(species.shape, jnp.float32)
    for kind in range(4):
        mass = mass + jnp.where(species == kind, MASSES[kind], 0.0).astype(jnp.float32)
    inv_mass = (1.0 / mass)[:, :, None, :]
    place = positions
    speed = velocities
    force = forces_all(place, species, neighbours, emb, params)
    for step in range(STEPS):
        speed = speed + 0.5 * TIME_STEP * inv_mass * force
        place = place + TIME_STEP * speed
        force = forces_all(place, species, neighbours, emb, params)
        speed = speed + 0.5 * TIME_STEP * inv_mass * force
    return (place, speed, force)
```

```python
import math

import jax
import jax.numpy as jnp
from jax import lax
from jax.experimental import pallas as pl
from jax.experimental.pallas import tpu as pltpu
from jax.sharding import PartitionSpec as P

MESH = pl.DeviceIdType.MESH
F32 = jnp.float32
BF16 = jnp.bfloat16

C = 64
HID = 128
EMB = 28
NBASIS = 8
NS = 4
SLOTS = 16
STEPS = 2
CENTERS = 8
NB = 16
LANES = 128
EVALS = STEPS + 1
GB = 4

TIME_STEP = 0.2
CUTOFF = 4.5
SOFTEN = 0.04
MASSES = (3.0, 2.0, 1.5, 1.0)

R3 = math.sqrt(3.0)
R5 = math.sqrt(5.0)
R15 = math.sqrt(15.0)


def dot(a, b):
    return jnp.dot(a, b, preferred_element_type=F32)


def iota(shape, dim):
    return lax.broadcasted_iota(jnp.int32, shape, dim)


def column(row, size):
    square = jnp.broadcast_to(row, (size, size))
    diag = jnp.where(iota((size, size), 0) == iota((size, size), 1), square, 0.0)
    return jnp.broadcast_to(jnp.sum(diag, axis=1, keepdims=True), (size, LANES))


def lane_pick(row, index):
    return jnp.take_along_axis(
        jnp.broadcast_to(row, index.shape), index, axis=1, mode="promise_in_bounds"
    )


def gate(x):
    sig = 0.5 * jnp.tanh(0.5 * x) + 0.5
    act = x * sig
    return act, sig * (1.0 + (x - act))


def kernel(
    nx, ny,
    pos_ref, vel_ref, kind_ref, nbr_ref, emb_ref, w_in_ref, w_two_ref, w_val_ref, w_env_ref,
    w_mix_ref, w_lat_ref, w_out_ref,
    pos_out, vel_out, frc_out,
    pbuf, psend, fbuf, fsend, onehot, slotmask, zrest, zfirst, geo, back, gdense,
    w_ve, w_ve_t, w_mix_t, w_two_t, w_in_t, w_hid_rows, w_hid_col, w_out_col, same, same16, seg,
    state, send_sem, recv_sem,
):
    mx, my = lax.axis_index("dx"), lax.axis_index("dy")
    others = [o for o in range(9) if o != 4]

    def device(o):
        p, q = o // 3 - 1, o % 3 - 1
        return (lax.rem(mx + (p + nx), nx), lax.rem(my + (q + ny), ny))

    barrier = pltpu.get_barrier_semaphore()
    for o in others:
        pl.semaphore_signal(barrier, inc=1, device_id=device(o), device_id_type=MESH)

    def pos_copy(t, o):
        return pltpu.make_async_remote_copy(
            src_ref=psend.at[t], dst_ref=pbuf.at[t, 8 - o],
            send_sem=send_sem.at[t, 0, o], recv_sem=recv_sem.at[t, 0, 8 - o],
            device_id=device(o), device_id_type=MESH,
        )

    def frc_copy(t, o):
        return pltpu.make_async_remote_copy(
            src_ref=fsend.at[t, o], dst_ref=fbuf.at[t, 8 - o],
            send_sem=send_sem.at[t, 1, o], recv_sem=recv_sem.at[t, 1, 8 - o],
            device_id=device(o), device_id_type=MESH,
        )

    kinds = kind_ref[0].astype(F32)
    start = jnp.concatenate([pos_ref[0, 0], kinds, jnp.zeros((4, LANES), F32)], axis=0)
    psend[0] = start
    state[0] = start
    state[1] = jnp.concatenate([vel_ref[0, 0], jnp.zeros((5, LANES), F32)], axis=0)
    pl.semaphore_wait(barrier, 8)
    for o in others:
        pos_copy(0, o).start()

    mass = jnp.zeros((1, LANES), F32)
    for kind in range(NS):
        mass = mass + jnp.where(kinds == float(kind), MASSES[kind], 0.0)
    inv_mass = 1.0 / mass

    w_ve[0 : 3 * C, :] = w_val_ref[...]
    w_ve[3 * C : 6 * C, :] = w_env_ref[...]
    w_ve_t[...] = jnp.concatenate(
        [w_val_ref[...].astype(F32), w_env_ref[...].astype(F32)], axis=0
    ).T.astype(BF16)
    w_mix_t[...] = w_mix_ref[...].astype(F32).T.astype(BF16)
    w_two_t[...] = w_two_ref[...].astype(F32).T.astype(BF16)
    w_in_t[...] = w_in_ref[...].astype(F32).T[0:16].astype(BF16)
    out_col = column(w_out_ref[...].reshape(1, C), C)
    w_out_col[...] = out_col
    w_hid = jnp.sum(w_lat_ref[...].astype(F32) * out_col, axis=0, keepdims=True)
    w_hid_col[...] = column(w_hid, HID)
    hid_hi = w_hid.astype(BF16).astype(F32)
    row16 = iota((16, LANES), 0)
    w_hid_rows[...] = jnp.where(
        row16 == 0, hid_hi, jnp.where(row16 == 1, w_hid - hid_hi, 0.0)
    ).astype(BF16)
    lane_r, lane_c = iota((LANES, LANES), 0), iota((LANES, LANES), 1)
    together = jnp.where(lane_r // SLOTS == lane_c // SLOTS, 1.0 / SLOTS, 0.0)
    same[...] = together
    same16[...] = together.astype(BF16)
    seg[...] = jnp.where(lane_r // SLOTS == lane_c % CENTERS, 1.0, 0.0).astype(BF16)

    nbrs = nbr_ref[0, 0]
    valid = jnp.where(nbrs >= 0, 1.0, 0.0)
    index = jnp.maximum(nbrs, 0)
    atom = jnp.bitwise_and(index, LANES - 1)
    slot = jnp.right_shift(index, 7)
    gdense[0] = atom.astype(F32)
    gdense[1] = slot.astype(F32)
    row_b, lane_b = iota((NB, LANES), 0), iota((NB, LANES), 1)
    centre_index = row_b * CENTERS + lane_b // SLOTS
    owner = jnp.where(lane_b // CENTERS == row_b, 1.0, 0.0)
    slot_x = (slot // 3).astype(F32) - 1.0
    slot_y = jnp.remainder(slot, 3).astype(F32) - 1.0

    def one_hots(b, carry):
        onehot[b] = jnp.where(
            lane_r.astype(F32) == gdense[0, pl.ds(b, 1), :], 1.0, 0.0
        ).astype(BF16)
        slotmask[b] = jnp.where(row16.astype(F32) == gdense[1, pl.ds(b, 1), :], 1.0, 0.0)
        return carry

    lax.fori_loop(0, NB, one_hots, 0)

    for o in others:
        pos_copy(0, o).wait_recv()
    pbuf[0, 4] = start
    far_kind = jnp.zeros((NB, LANES), F32)
    for o in range(9):
        far_kind = jnp.where(slot == o, lane_pick(pbuf[0, o, 3:4, :], atom), far_kind)
    gdense[0] = lane_pick(kinds, centre_index)
    gdense[1] = far_kind
    emb_t = emb_ref[...].astype(F32).T.astype(BF16)
    row4 = iota((NS, LANES), 0).astype(F32)

    def embeddings(b, carry):
        looked = [
            dot(emb_t, jnp.where(row4 == gdense[i, pl.ds(b, 1), :], 1.0, 0.0).astype(BF16))
            for i in range(2)
        ]
        both = jnp.concatenate(looked, axis=0)
        zfirst[b] = both[0:8]
        zrest[b] = both[8 : 2 * EMB].astype(BF16)
        return carry

    lax.fori_loop(0, NB, embeddings, 0)

    row8 = iota((8, LANES), 0)

    def group(g, carry):
        blocks = [g * GB + j for j in range(GB)]

        def wide(parts):
            return jnp.concatenate(parts, axis=1)

        def part(x, j):
            return x[:, j * LANES : (j + 1) * LANES]

        cut = wide([geo[b, 16:17, :] for b in blocks])
        top = wide([jnp.concatenate([geo[b, 0:8, :], zfirst[b]], axis=0) for b in blocks])
        zin = jnp.concatenate([top.astype(BF16), wide([zrest[b] for b in blocks])], axis=0)
        hidden, slope1 = gate(dot(w_in_ref[...], zin))
        pre = dot(w_two_ref[...], hidden.astype(BF16))
        latent16 = (pre * cut).astype(BF16)
        value_envw = dot(w_ve[...], latent16)
        value = value_envw[0 : 3 * C]
        envw = value_envw[3 * C : 6 * C].astype(BF16)

        gram = []
        sphs = []
        for b in blocks:
            sph = geo[b, 8:16, :]
            tall = sph.T.astype(BF16)
            g1 = dot(tall, jnp.where(row8 < 3, sph, 0.0).astype(BF16))
            g2 = dot(tall, jnp.where(row8 < 3, 0.0, sph).astype(BF16))
            sphs.append(sph.astype(BF16))
            gram.append(
                [same16[...], (g1 * same[...]).astype(BF16), (g2 * same[...]).astype(BF16)]
            )

        def mix_slots(x):
            return wide(
                [
                    jnp.concatenate(
                        [dot(part(x, j)[l * C : (l + 1) * C], gram[j][l]) for l in range(3)], axis=0
                    )
                    for j in range(GB)
                ]
            )

        env_at = mix_slots(envw)
        mixed = jnp.concatenate([latent16, (value * env_at).astype(BF16)], axis=0)
        hidden2, slope2 = gate(dot(w_mix_ref[...], mixed))
        readout = dot(w_hid_rows[...], hidden2.astype(BF16))
        readout = readout[0:1] + readout[1:2]

        d_a2 = slope2 * (wide([w_hid_col[...]] * GB) * cut)
        d_mixed = dot(w_mix_t[...], d_a2.astype(BF16))
        d_scal = d_mixed[C : 4 * C]
        d_value = (d_scal * env_at).astype(BF16)
        d_envat = (d_scal * value).astype(BF16)
        d_envw = mix_slots(d_envat).astype(BF16)
        energy_part = wide([w_out_col[...]] * GB) * cut
        d_latent = d_mixed[0:C] + dot(
            w_ve_t[...], jnp.concatenate([d_value, d_envw], axis=0)
        ) + energy_part
        d_cut = readout + jnp.sum(pre * (d_latent + energy_part), axis=0, keepdims=True)
        d_hidden = dot(w_two_t[...], (d_latent * cut).astype(BF16))
        d_basis = dot(w_in_t[...], (d_hidden * slope1).astype(BF16))

        for j, b in enumerate(blocks):
            d_sph = []
            for l in (1, 2):
                dq, ew = part(d_envat, j)[l * C : (l + 1) * C], part(envw, j)[l * C : (l + 1) * C]
                left, right = jnp.concatenate([dq, ew], axis=0), jnp.concatenate([ew, dq], axis=0)
                pair = lax.dot_general(
                    left, right, (((0,), (0,)), ((), ())), preferred_element_type=F32
                )
                d_sph.append(dot(sphs[j], (pair * same[...]).astype(BF16)))
            back[b, 0:8, :] = part(d_basis, j)[0:8]
            back[b, 8:16, :] = jnp.where(row8 < 3, d_sph[0], d_sph[1])
            back[b, 16:17, :] = part(d_cut, j)
        return carry

    def evaluate(t, carry):
        @pl.when(t > 0)
        def _():
            psend[t] = state[0]
            for o in others:
                pos_copy(t, o).start()
            for o in others:
                pos_copy(t, o).wait_recv()
            pbuf[t, 4] = state[0]

        here = state[0]
        rel = []
        for k in range(3):
            far = jnp.zeros((NB, LANES), F32)
            for o in range(9):
                far = jnp.where(slot == o, lane_pick(pbuf[t, o, k : k + 1, :], atom), far)
            if k == 0:
                far = far + slot_x
            if k == 1:
                far = far + slot_y
            rel.append(far - lane_pick(here[k : k + 1], centre_index))
        dist_sq = rel[0] * rel[0] + rel[1] * rel[1] + rel[2] * rel[2] + SOFTEN
        dist = jnp.sqrt(dist_sq)
        inv = 1.0 / dist
        ux, uy, uz = rel[0] * inv, rel[1] * inv, rel[2] * inv
        fall = 1.0 - dist_sq * (1.0 / (CUTOFF * CUTOFF))
        cut = valid * fall * fall
        theta = dist * (math.pi / CUTOFF)
        sin1, cos1 = jnp.sin(theta), jnp.cos(theta)
        sines, cosines = [sin1], [cos1]
        for n in range(1, NBASIS):
            s, c = sines[-1], cosines[-1]
            sines.append(s * cos1 + c * sin1)
            cosines.append(c * cos1 - s * sin1)
        for n in range(NBASIS):
            geo[:, n, :] = sines[n] * inv * cut
        sph = (
            R3 * ux, R3 * uy, R3 * uz, R15 * ux * uy, R15 * uy * uz,
            0.5 * R5 * (3.0 * uz * uz - 1.0), R15 * ux * uz, 0.5 * R15 * (ux * ux - uy * uy),
        )
        for m in range(8):
            geo[:, 8 + m, :] = sph[m]
        geo[:, 16, :] = cut

        lax.fori_loop(0, NB // GB, group, 0)

        d1, d2, d3, d4, d5, d6, d7, d8 = [back[:, 8 + m, :] for m in range(8)]
        du = (
            R3 * d1 + R15 * (uy * d4 + uz * d7 + ux * d8),
            R3 * d2 + R15 * (ux * d4 + uz * d5 - uy * d8),
            R3 * d3 + R15 * (uy * d5 + ux * d7) + (3.0 * R5) * (uz * d6),
        )
        by_sin = jnp.zeros((NB, LANES), F32)
        by_cos = jnp.zeros((NB, LANES), F32)
        for n in range(NBASIS):
            d_basis = back[:, n, :]
            by_sin = by_sin + d_basis * sines[n]
            by_cos = by_cos + (d_basis * cosines[n]) * ((n + 1) * math.pi / CUTOFF)
        by_sin = by_sin * inv
        d_cut = back[:, 16, :] + by_sin
        d_dist = cut * inv * (by_cos - by_sin) - inv * (du[0] * ux + du[1] * uy + du[2] * uz)
        d_sq = 0.5 * inv * d_dist - d_cut * (valid * fall) * (2.0 / (CUTOFF * CUTOFF))
        grads = [(du[k] * inv + 2.0 * rel[k] * d_sq) * valid for k in range(3)]

        split = []
        for k in range(3):
            high = grads[k].astype(BF16).astype(F32)
            gdense[k] = high
            gdense[3 + k] = grads[k] - high
        segs = dot(gdense[...].reshape(6 * NB, LANES).astype(BF16), seg[...])
        centre = [
            jnp.sum(
                (segs[k * NB : (k + 1) * NB] + segs[(3 + k) * NB : (4 + k) * NB]) * owner,
                axis=0, keepdims=True,
            )
            for k in range(3)
        ]
        scattered = jnp.zeros((6 * 16, LANES), F32)
        for b in range(NB):
            left = jnp.concatenate(
                [gdense[i, b : b + 1, :] * slotmask[b] for i in range(6)], axis=0
            ).astype(BF16)
            scattered = scattered + lax.dot_general(
                left, onehot[b], (((1,), (1,)), ((), ())), preferred_element_type=F32
            )
        ghost = [
            scattered[k * 16 : (k + 1) * 16] + scattered[(3 + k) * 16 : (4 + k) * 16]
            for k in range(3)
        ]
        for k in range(3):
            fsend[t, :, k, :] = ghost[k][0:9]
        for o in others:
            frc_copy(t, o).start()
        own = jnp.concatenate(
            [centre[k] - ghost[k][4:5] for k in range(3)] + [jnp.zeros((5, LANES), F32)], axis=0
        )
        for o in others:
            frc_copy(t, o).wait_recv()
        back_sum = fbuf[t, 0]
        for o in others[1:]:
            back_sum = back_sum + fbuf[t, o]
        force = jnp.where(row8 < 3, own - back_sum, 0.0)

        half = (0.5 * TIME_STEP) * inv_mass
        speed = state[1]
        speed = speed + jnp.where(t > 0, 1.0, 0.0) * (half * force)
        more = jnp.where(t < STEPS, 1.0, 0.0)
        speed = speed + more * (half * force)
        state[1] = speed
        state[0] = here + (more * TIME_STEP) * speed
        state[2] = force
        for o in others:
            pos_copy(t, o).wait_send()
            frc_copy(t, o).wait_send()
        return carry

    lax.fori_loop(0, EVALS, evaluate, 0)
    pos_out[0, 0] = state[0, 0:3, :]
    vel_out[0, 0] = state[1, 0:3, :]
    frc_out[0, 0] = state[2, 0:3, :]


def solution(mesh):
    nx, ny = mesh.shape["dx"], mesh.shape["dy"]

    def per_device(*args):
        def body(*refs):
            kernel(nx, ny, *refs)

        vmem = pl.BlockSpec(memory_space=pltpu.VMEM)
        out = jax.ShapeDtypeStruct((1, 1, 3, LANES), F32)
        return pl.pallas_call(
            body,
            out_shape=(out, out, out),
            in_specs=[vmem] * len(args),
            out_specs=(vmem, vmem, vmem),
            scratch_shapes=[
                pltpu.VMEM((EVALS, 9, 8, LANES), F32),
                pltpu.VMEM((EVALS, 8, LANES), F32),
                pltpu.VMEM((EVALS, 9, 8, LANES), F32),
                pltpu.VMEM((EVALS, 9, 8, LANES), F32),
                pltpu.VMEM((NB, LANES, LANES), BF16),
                pltpu.VMEM((NB, 16, LANES), F32),
                pltpu.VMEM((NB, 48, LANES), BF16),
                pltpu.VMEM((NB, 8, LANES), F32),
                pltpu.VMEM((NB, 24, LANES), F32),
                pltpu.VMEM((NB, 24, LANES), F32),
                pltpu.VMEM((6, NB, LANES), F32),
                pltpu.VMEM((6 * C, C), BF16),
                pltpu.VMEM((C, 6 * C), BF16),
                pltpu.VMEM((4 * C, HID), BF16),
                pltpu.VMEM((HID, C), BF16),
                pltpu.VMEM((16, HID), BF16),
                pltpu.VMEM((16, HID), BF16),
                pltpu.VMEM((HID, LANES), F32),
                pltpu.VMEM((C, LANES), F32),
                pltpu.VMEM((LANES, LANES), F32),
                pltpu.VMEM((LANES, LANES), BF16),
                pltpu.VMEM((LANES, LANES), BF16),
                pltpu.VMEM((3, 8, LANES), F32),
                pltpu.SemaphoreType.DMA((EVALS, 2, 9)),
                pltpu.SemaphoreType.DMA((EVALS, 2, 9)),
            ],
            compiler_params=pltpu.CompilerParams(
                collective_id=0, has_side_effects=True, vmem_limit_bytes=48 * 1024 * 1024
            ),
        )(*args)

    grid4 = P("dx", "dy", None, None)
    in_specs = (grid4, grid4, P("dx", "dy", None), grid4) + (P(),) * 8
    return jax.shard_map(
        per_device, mesh=mesh, in_specs=in_specs, out_specs=(grid4, grid4, grid4), check_vma=False
    )
```

```python
import math

import jax
import jax.numpy as jnp
from jax import lax
from jax.experimental import pallas as pl
from jax.experimental.pallas import tpu as pltpu
from jax.sharding import PartitionSpec as P

MESH = pl.DeviceIdType.MESH
F32 = jnp.float32
BF16 = jnp.bfloat16

C = 64
HID = 128
EMB = 28
NBASIS = 8
NS = 4
SLOTS = 16
STEPS = 2
CENTERS = 8
NB = 16
LANES = 128
EVALS = STEPS + 1
GB = 8
LAG = 0

VMEM_BYTES = 63 * 1024 * 1024

TIME_STEP = 0.2
CUTOFF = 4.5
SOFTEN = 0.04
MASSES = (3.0, 2.0, 1.5, 1.0)

R3 = math.sqrt(3.0)
R5 = math.sqrt(5.0)
R15 = math.sqrt(15.0)


def dot(a, b):
    return jnp.dot(a, b, preferred_element_type=F32)


def iota(shape, dim):
    return lax.broadcasted_iota(jnp.int32, shape, dim)


def column(row, size):
    square = jnp.broadcast_to(row, (size, size))
    diag = jnp.where(iota((size, size), 0) == iota((size, size), 1), square, 0.0)
    return jnp.broadcast_to(jnp.sum(diag, axis=1, keepdims=True), (size, LANES))


def lane_pick(row, index):
    return jnp.take_along_axis(
        jnp.broadcast_to(row, index.shape), index, axis=1, mode="promise_in_bounds"
    )


def gate(half):
    t = jnp.tanh(half)
    up = 1.0 + t
    act = half * up
    return act.astype(BF16), (up + act * (1.0 - t)).astype(BF16)


def kernel(
    nx, ny,
    pos_hbm, vel_hbm, kind_hbm, nbr_hbm, emb_hbm, w_in_hbm, w_two_hbm, w_val_hbm, w_env_hbm,
    w_mix_hbm, w_lat_hbm, w_out_hbm,
    pos_out, vel_out, frc_out,
    pbuf, psend, fbuf, gbuf, fsend, onehot, slotmask, zrest, zfirst, geo, back, spread, gdense, halves,
    w_in_half, w_mix_half, w_ve, w_ve_t, w_mix_t, w_two_t, w_in_t, w_hid_rows, w_out_col, same2,
    same16, seg,
    pos_ref, vel_ref, kind_ref, nbr_ref, emb_ref, w_in_ref, w_two_ref, w_val_ref, w_env_ref,
    w_mix_ref, w_lat_ref, w_out_ref,
    pos_sems, frc_sems, own_sems, load_sems,
):
    loads = [
        pltpu.make_async_copy(src, dst, load_sems.at[i])
        for i, (src, dst) in enumerate(
            (
                (pos_hbm, pos_ref), (vel_hbm, vel_ref), (kind_hbm, kind_ref), (nbr_hbm, nbr_ref),
                (emb_hbm, emb_ref), (w_in_hbm, w_in_ref), (w_two_hbm, w_two_ref),
                (w_val_hbm, w_val_ref), (w_env_hbm, w_env_ref), (w_mix_hbm, w_mix_ref),
                (w_lat_hbm, w_lat_ref), (w_out_hbm, w_out_ref),
            )
        )
    ]
    for load in loads:
        load.start()
    mx, my = lax.axis_index("dx"), lax.axis_index("dy")
    near = [(p, q) for p in (-1, 0, 1) for q in (-1, 0, 1) if (p, q) != (0, 0)]
    wide_area = [
        (p, q) for p in range(-2, 3) for q in range(-2, 3) if (p, q) != (0, 0)
    ]

    def device(p, q):
        return (lax.rem(mx + (p + nx), nx), lax.rem(my + (q + ny), ny))

    barrier = pltpu.get_barrier_semaphore()
    for p, q in wide_area:
        pl.semaphore_signal(barrier, inc=1, device_id=device(p, q), device_id_type=MESH)

    def pos_copy(p, q):
        here, there = 3 * (p + 1) + q + 1, 3 * (1 - p) + 1 - q
        return pltpu.make_async_remote_copy(
            src_ref=psend, dst_ref=pbuf.at[there],
            send_sem=pos_sems.at[0, here], recv_sem=pos_sems.at[1, there],
            device_id=device(p, q), device_id_type=MESH,
        )

    def frc_copy(t, p, q):
        here, there = 5 * (p + 2) + q + 2, 5 * (2 - p) + 2 - q

        def box(ref, dp, dq):
            low_p, low_q = max(-1, p - 1), max(-1, q - 1)
            return ref.at[
                pl.ds(low_p - dp + 1, 3 - abs(p)), pl.ds(low_q - dq + 1, 3 - abs(q))
            ]

        return pltpu.make_async_remote_copy(
            src_ref=box(fsend.at[t], 0, 0), dst_ref=box(gbuf.at[t, there], p, q),
            send_sem=frc_sems.at[0, t, here], recv_sem=frc_sems.at[1, t, there],
            device_id=device(p, q), device_id_type=MESH,
        )

    def own_copy(p, q):
        here, there = 3 * (p + 1) + q + 1, 3 * (1 - p) + 1 - q
        return pltpu.make_async_remote_copy(
            src_ref=fsend.at[STEPS, p + 1, q + 1], dst_ref=fbuf.at[there],
            send_sem=own_sems.at[0, here], recv_sem=own_sems.at[1, there],
            device_id=device(p, q), device_id_type=MESH,
        )

    for load in loads[0:3]:
        load.wait()
    kinds = kind_ref[0].astype(F32)
    start = jnp.concatenate(
        [pos_ref[0, :, 0, :], kinds, vel_ref[0, :, 0, :], jnp.zeros((1, LANES), F32)], axis=0
    )
    psend[...] = start
    pl.semaphore_wait(barrier, len(wide_area))
    for p, q in near:
        pos_copy(p, q).start()

    pbuf[4] = start
    fsend[...] = jnp.zeros(fsend.shape, F32)

    def inv_mass(kind):
        mass = jnp.zeros((1, LANES), F32)
        for k in range(NS):
            mass = mass + jnp.where(kind == float(k), MASSES[k], 0.0)
        return 1.0 / mass

    for load in loads[3:]:
        load.wait()
    val_t, env_t = w_val_ref[...].astype(F32), w_env_ref[...].astype(F32)
    w_ve[0 : 3 * C, :] = val_t.T.astype(BF16)
    w_ve[3 * C : 6 * C, :] = env_t.T.astype(BF16)
    w_ve_t[...] = jnp.concatenate([val_t, env_t], axis=1).astype(BF16)
    w_in_half[...] = (0.5 * w_in_ref[...].astype(F32).T).astype(BF16)
    w_mix_half[...] = (0.5 * w_mix_ref[...].astype(F32)).astype(BF16)
    w_two_t[...] = (0.5 * w_two_ref[...].astype(F32).T).astype(BF16)
    w_in_t[...] = w_in_ref[0:16]
    out_col = column(w_out_ref[...].reshape(1, C), C)
    w_out_col[...] = out_col
    w_hid = jnp.sum(w_lat_ref[...].astype(F32) * out_col, axis=0, keepdims=True)
    w_hid_col = column(w_hid, HID)
    w_mix_t[...] = (
        (0.5 * w_mix_ref[...].astype(F32)) * jnp.concatenate([w_hid_col] * 2, axis=1)
    ).T.astype(BF16)
    hid_hi = w_hid.astype(BF16).astype(F32)
    row16 = iota((16, LANES), 0)
    w_hid_rows[...] = jnp.where(
        row16 == 0, hid_hi, jnp.where(row16 == 1, w_hid - hid_hi, 0.0)
    ).astype(BF16)
    lane_r, lane_c = iota((LANES, LANES), 0), iota((LANES, LANES), 1)
    together = jnp.where(lane_r // SLOTS == lane_c // SLOTS, 1.0 / SLOTS, 0.0)
    same16[...] = together.astype(BF16)
    pair_r, pair_c = iota((2 * LANES, 2 * LANES), 0), iota((2 * LANES, 2 * LANES), 1)
    same2[...] = jnp.where(pair_r // SLOTS == pair_c // SLOTS, 1.0 / SLOTS, 0.0).astype(BF16)
    seg[...] = jnp.where(lane_r // SLOTS == lane_c % CENTERS, 1.0, 0.0).astype(BF16)

    nbrs = nbr_ref[0, 0]
    valid = jnp.where(nbrs >= 0, 1.0, 0.0)
    index = jnp.maximum(nbrs, 0)
    atom = jnp.bitwise_and(index, LANES - 1)
    slot = jnp.right_shift(index, 7)
    gdense[0] = atom.astype(F32)
    gdense[1] = slot.astype(F32)
    row_b, lane_b = iota((NB, LANES), 0), iota((NB, LANES), 1)
    centre_index = row_b * CENTERS + lane_b // SLOTS
    owner = jnp.where(lane_b // CENTERS == row_b, 1.0, 0.0)
    slot_x = (slot // 3).astype(F32) - 1.0
    slot_y = jnp.remainder(slot, 3).astype(F32) - 1.0

    def one_hots(i, carry):
        for j in range(2):
            b = 2 * i + j
            onehot[i, :, j * LANES : (j + 1) * LANES] = jnp.where(
                lane_r.astype(F32) == gdense[0, pl.ds(b, 1), :], 1.0, 0.0
            ).astype(BF16)
            slotmask[b] = jnp.where(row16.astype(F32) == gdense[1, pl.ds(b, 1), :], 1.0, 0.0)
        return carry

    lax.fori_loop(0, NB // 2, one_hots, 0)

    row8 = iota((8, LANES), 0)
    emb_t = emb_ref[...].astype(F32).T
    blank = jnp.zeros((EMB, NS), F32)
    emb_both = jnp.concatenate(
        [jnp.concatenate([emb_t, blank], axis=1), jnp.concatenate([blank, emb_t], axis=1)], axis=0
    ).astype(BF16)

    for p, q in near:
        pos_copy(p, q).wait_recv()
    far_kind = jnp.zeros((NB, LANES), F32)
    for o in range(9):
        far_kind = jnp.where(slot == o, lane_pick(pbuf[o, 3:4, :], atom), far_kind)
    for o in range(9):
        halves[o] = jnp.broadcast_to(
            (0.5 * TIME_STEP) * inv_mass(pbuf[o, 3:4, :]), (8, LANES)
        )
    gdense[0] = lane_pick(kinds, centre_index)
    gdense[1] = far_kind
    kind_of = jnp.where(row8 < NS, row8, row8 - NS).astype(F32)
    chosen = jnp.concatenate(
        [
            jnp.where(
                kind_of == jnp.where(row8 < NS, gdense[0, b : b + 1, :], gdense[1, b : b + 1, :]),
                1.0, 0.0,
            ).astype(BF16)
            for b in range(NB)
        ],
        axis=1,
    )
    looked = dot(emb_both, chosen)
    for b in range(NB):
        zfirst[b] = looked[0:8, b * LANES : (b + 1) * LANES]
        zrest[b] = looked[8 : 2 * EMB, b * LANES : (b + 1) * LANES].astype(BF16)

    slot_lane = lane_b // SLOTS * SLOTS + row_b
    lane_atom = lane_b // SLOTS

    def wide(parts):
        return jnp.concatenate(parts, axis=1)

    def tall(parts):
        return jnp.concatenate(parts, axis=0)

    def part(x, j):
        return x[:, j * LANES : (j + 1) * LANES]

    def order(x, l):
        return x[l * C : (l + 1) * C]

    def corner(a, b):
        zero = jnp.zeros((LANES, LANES), BF16)
        return tall([wide([a, zero]), wide([zero, b])])

    def chain(tiles):
        count = len(tiles)
        each = range(count)

        def gather(values):
            return [[] for _ in range(values)]

        def mix_slots(x, gram):
            first = dot(tall([order(x[i], 0) for i in each]), same2[...]).astype(BF16)
            yield None
            mixed = []
            for i in each:
                mixed.append(
                    tall(
                        [order(first, i)]
                        + [dot(order(x[i], l), gram[i][l - 1]).astype(BF16) for l in (1, 2)]
                    )
                )
                yield None
            yield mixed

        cut, cut16, a1, hidden, slope1, pre, latent16, value, envw, a2, hidden2, slope2 = gather(12)
        d_a2, readout, d_mixed, d_value, d_envat, d_latent, d_hidden, picks, gram = gather(9)
        for i in each:
            pair = (2 * tiles[i], 2 * tiles[i] + 1)
            cut.append(wide([geo[b, 16:17, :] for b in pair]))
            cut16.append(cut[i].astype(BF16))
            top = wide([tall([geo[b, 0:8, :], zfirst[b]]) for b in pair])
            zin = tall([top.astype(BF16), wide([zrest[b] for b in pair])])
            a1.append(dot(w_in_half[...], zin))
            yield
        for i in each:
            act, slope = gate(a1[i])
            hidden.append(act)
            slope1.append(slope)
            yield
        for i in each:
            pre.append(dot(w_two_ref[...], hidden[i]))
            latent16.append((pre[i] * cut[i]).astype(BF16))
            yield
        for i in each:
            blockwise = []
            for b in (2 * tiles[i], 2 * tiles[i] + 1):
                sph = geo[b, 8:16, :]
                rows = [sph[m : m + 1] for m in range(8)]
                far = [lane_pick(row, slot_lane) for row in rows]
                terms = [far[m] * rows[m] for m in range(8)]
                compact = [
                    (terms[0] + terms[1]) + terms[2],
                    ((terms[3] + terms[4]) + (terms[5] + terms[6])) + terms[7],
                ]
                picks.append(far)
                blockwise.append([tall([x.astype(BF16)] * CENTERS) * same16[...] for x in compact])
            gram.append([corner(blockwise[0][l], blockwise[1][l]) for l in range(2)])
            yield
        for i in each:
            value_envw = dot(w_ve[...], latent16[i])
            value.append(value_envw[0 : 3 * C].astype(BF16))
            envw.append(value_envw[3 * C : 6 * C].astype(BF16))
            yield
        for env_at in mix_slots(envw, gram):
            if env_at is None:
                yield
        for i in each:
            mixed = tall([latent16[i], value[i] * env_at[i]])
            a2.append(dot(w_mix_half[...], mixed))
            yield
        for i in each:
            act, slope = gate(a2[i])
            hidden2.append(act)
            d_a2.append(slope * cut16[i])
            yield
        for i in each:
            d_mixed.append(dot(w_mix_t[...], d_a2[i]))
            d_scal = d_mixed[i][C : 4 * C].astype(BF16)
            d_value.append(d_scal * env_at[i])
            d_envat.append(d_scal * value[i])
            yield
        for i in each:
            for j in range(2):
                dq, ew = part(d_envat[i], j), part(envw[i], j)
                left = tall([order(dq, 1), order(ew, 1), order(dq, 2), order(ew, 2)])
                right = corner(
                    tall([order(ew, 1), order(dq, 1)]), tall([order(ew, 2), order(dq, 2)])
                )
                pair = lax.dot_general(
                    left, right, (((0,), (0,)), ((), ())), preferred_element_type=F32
                )
                sums = []
                for l in range(2):
                    full = part(pair, l)
                    own = full[0:SLOTS]
                    for a in range(1, CENTERS):
                        own = jnp.where(
                            lane_atom == a, full[a * SLOTS : (a + 1) * SLOTS], own
                        )
                    sums.append(own)
                for m in range(8):
                    product = sums[0 if m < 3 else 1] * picks[2 * i + j][m]
                    spread[m, 2 * tiles[i] + j] = product[0:8] + product[8:16]
                yield
        for d_envw in mix_slots(d_envat, gram):
            if d_envw is None:
                yield
        for i in each:
            both = dot(w_hid_rows[...], hidden2[i])
            readout.append(both[0:1] + both[1:2])
            energy_part = wide([w_out_col[...]] * 2) * cut[i]
            rest = dot(w_ve_t[...], tall([d_value[i], d_envw[i]]))
            d_latent.append((d_mixed[i][0:C] + rest) + energy_part)
            d_cut = readout[i] + jnp.sum(
                pre[i] * (d_latent[i] + energy_part), axis=0, keepdims=True
            )
            for j in range(2):
                back[2 * tiles[i] + j, 8:9, :] = part(d_cut, j)
            yield
        for i in each:
            d_hidden.append(dot(w_two_t[...], (d_latent[i] * cut[i]).astype(BF16)).astype(BF16))
            yield
        for i in each:
            d_basis = dot(w_in_t[...], d_hidden[i] * slope1[i])
            for j in range(2):
                back[2 * tiles[i] + j, 0:8, :] = part(d_basis, j)[0:8]
            yield

    def run_chains(lag):
        waiting = [chain(list(range(i, i + GB // 2))) for i in range(0, NB // 2, GB // 2)]
        running = []
        step = 0
        while waiting or running:
            while waiting and (lag == 0 or step % lag == 0):
                running.append(waiting.pop(0))
                if lag:
                    break
            for one in list(running):
                if next(one, 0) == 0:
                    running.remove(one)
            step += 1

    far_first = sorted(wide_area, key=lambda o: (abs(o[0]) + abs(o[1]), o))
    middle = iota((3, LANES), 0) == 1

    def evaluate(t, carry):
        here = pbuf[4]
        rel = []
        for k in range(3):
            far = jnp.zeros((NB, LANES), F32)
            for o in range(9):
                far = jnp.where(slot == o, lane_pick(pbuf[o, k : k + 1, :], atom), far)
            if k == 0:
                far = far + slot_x
            if k == 1:
                far = far + slot_y
            rel.append(far - lane_pick(here[k : k + 1], centre_index))
        dist_sq = rel[0] * rel[0] + rel[1] * rel[1] + rel[2] * rel[2] + SOFTEN
        dist = jnp.sqrt(dist_sq)
        inv = 1.0 / dist
        ux, uy, uz = rel[0] * inv, rel[1] * inv, rel[2] * inv
        fall = 1.0 - dist_sq * (1.0 / (CUTOFF * CUTOFF))
        cut = valid * fall * fall
        theta = dist * (math.pi / CUTOFF)
        sin1, cos1 = jnp.sin(theta), jnp.cos(theta)
        sines, cosines = [sin1], [cos1]
        for n in range(1, NBASIS):
            s, c = sines[-1], cosines[-1]
            sines.append(s * cos1 + c * sin1)
            cosines.append(c * cos1 - s * sin1)
        for n in range(NBASIS):
            geo[:, n, :] = sines[n] * inv * cut
        sph = (
            R3 * ux, R3 * uy, R3 * uz, R15 * ux * uy, R15 * uy * uz,
            0.5 * R5 * (3.0 * uz * uz - 1.0), R15 * ux * uz, 0.5 * R15 * (ux * ux - uy * uy),
        )
        for m in range(8):
            geo[:, 8 + m, :] = sph[m]
        geo[:, 16, :] = cut

        run_chains(LAG)

        d_sph = []
        for m in range(8):
            parts = [spread[m, :, i, :] for i in range(8)]
            total = ((parts[0] + parts[1]) + (parts[2] + parts[3])) + (
                (parts[4] + parts[5]) + (parts[6] + parts[7])
            )
            d_sph.append(total * (1.0 / SLOTS))
        d1, d2, d3, d4, d5, d6, d7, d8 = d_sph
        du = (
            R3 * d1 + R15 * (uy * d4 + uz * d7 + ux * d8),
            R3 * d2 + R15 * (ux * d4 + uz * d5 - uy * d8),
            R3 * d3 + R15 * (uy * d5 + ux * d7) + (3.0 * R5) * (uz * d6),
        )
        by_sin = jnp.zeros((NB, LANES), F32)
        by_cos = jnp.zeros((NB, LANES), F32)
        for n in range(NBASIS):
            d_basis = back[:, n, :]
            by_sin = by_sin + d_basis * sines[n]
            by_cos = by_cos + (d_basis * cosines[n]) * ((n + 1) * math.pi / CUTOFF)
        by_sin = by_sin * inv
        d_cut = back[:, 8, :] + by_sin
        d_dist = cut * inv * (by_cos - by_sin) - inv * (du[0] * ux + du[1] * uy + du[2] * uz)
        d_sq = 0.5 * inv * d_dist - d_cut * (valid * fall) * (2.0 / (CUTOFF * CUTOFF))
        grads = [(du[k] * inv + 2.0 * rel[k] * d_sq) * valid for k in range(3)]

        split = []
        for k in range(3):
            high = grads[k].astype(BF16).astype(F32)
            gdense[k] = high
            gdense[3 + k] = grads[k] - high
        segs = dot(gdense[...].reshape(6 * NB, LANES).astype(BF16), seg[...])
        centre = [
            jnp.sum(
                (segs[k * NB : (k + 1) * NB] + segs[(3 + k) * NB : (4 + k) * NB]) * owner,
                axis=0, keepdims=True,
            )
            for k in range(3)
        ]
        sums = [jnp.zeros((6 * 16, LANES), F32)] * 2
        for i in range(NB // 2):
            left = wide(
                [
                    tall([gdense[k, b : b + 1, :] * slotmask[b] for k in range(6)]).astype(BF16)
                    for b in (2 * i, 2 * i + 1)
                ]
            )
            sums[i % 2] = sums[i % 2] + lax.dot_general(
                left, onehot[i], (((1,), (1,)), ((), ())), preferred_element_type=F32
            )
        scattered = sums[0] + sums[1]
        ghost = [
            scattered[k * 16 : (k + 1) * 16] + scattered[(3 + k) * 16 : (4 + k) * 16]
            for k in range(3)
        ]
        for k in range(3):
            for p in range(3):
                terms = -ghost[k][3 * p : 3 * p + 3]
                if p == 1:
                    terms = terms + jnp.where(middle, centre[k], 0.0)
                fsend[t, p, :, k, :] = terms

        @pl.when(t < STEPS)
        def _():
            for p, q in reversed(far_first):
                frc_copy(t, p, q).start()
            for p, q in far_first:
                frc_copy(t, p, q).wait_recv()
            for dp in range(-1, 2):
                for dq in range(-1, 2):
                    force = fsend[t, dp + 1, dq + 1]
                    for a in range(dp - 1, dp + 2):
                        for b in range(dq - 1, dq + 2):
                            if (a, b) != (0, 0):
                                force = force + gbuf[t, 5 * (a + 2) + b + 2, dp + 1, dq + 1]
                    slot_at = 3 * (dp + 1) + dq + 1
                    kick = halves[slot_at, 0:1, :] * force[0:3]
                    speed = pbuf[slot_at, 4:7, :]
                    speed = speed + jnp.where(t > 0, 1.0, 0.0) * kick
                    speed = speed + kick
                    pbuf[slot_at, 4:7, :] = speed
                    pbuf[slot_at, 0:3, :] = pbuf[slot_at, 0:3, :] + TIME_STEP * speed
            for p, q in far_first:
                frc_copy(t, p, q).wait_send()

        return carry

    lax.fori_loop(0, EVALS, evaluate, 0)
    for p, q in near:
        own_copy(p, q).start()
    for p, q in near:
        pos_copy(p, q).wait_send()
    for p, q in near:
        own_copy(p, q).wait_recv()
    force = fsend[STEPS, 1, 1]
    for p, q in near:
        force = force + fbuf[3 * (p + 1) + q + 1]
    speed = pbuf[4, 4:7, :] + halves[4, 0:1, :] * force[0:3]
    pos_out[0, :, 0, :] = pbuf[4, 0:3, :]
    vel_out[0, :, 0, :] = speed
    frc_out[0, :, 0, :] = force[0:3]
    for p, q in near:
        own_copy(p, q).wait_send()


def solution(mesh):
    nx, ny = mesh.shape["dx"], mesh.shape["dy"]

    def per_device(positions, velocities, species, neighbours, emb, w_in, w_two, w_val, w_env, *more):
        rows = (0, 2, 1, 3)
        args = (
            positions.transpose(rows), velocities.transpose(rows), species, neighbours, emb,
            w_in.T, w_two, w_val.T, w_env.T, *more,
        )

        def body(*refs):
            kernel(nx, ny, *refs)

        vmem = pl.BlockSpec(memory_space=pltpu.VMEM)
        out = jax.ShapeDtypeStruct((1, 3, 1, LANES), F32)
        results = pl.pallas_call(
            body,
            out_shape=(out, out, out),
            in_specs=[pl.BlockSpec(memory_space=pltpu.HBM)] * len(args),
            out_specs=(vmem, vmem, vmem),
            scratch_shapes=[
                pltpu.VMEM((9, 8, LANES), F32),
                pltpu.VMEM((8, LANES), F32),
                pltpu.VMEM((9, 4, LANES), F32),
                pltpu.VMEM((STEPS, 25, 3, 3, 4, LANES), F32),
                pltpu.VMEM((EVALS, 3, 3, 4, LANES), F32),
                pltpu.VMEM((NB // 2, LANES, 2 * LANES), BF16),
                pltpu.VMEM((NB, 16, LANES), F32),
                pltpu.VMEM((NB, 48, LANES), BF16),
                pltpu.VMEM((NB, 8, LANES), F32),
                pltpu.VMEM((NB, 24, LANES), F32),
                pltpu.VMEM((NB, 16, LANES), F32),
                pltpu.VMEM((8, NB, 8, LANES), F32),
                pltpu.VMEM((6, NB, LANES), F32),
                pltpu.VMEM((9, 8, LANES), F32),
                pltpu.VMEM((HID, NBASIS + 2 * EMB), BF16),
                pltpu.VMEM((HID, 4 * C), BF16),
                pltpu.VMEM((6 * C, C), BF16),
                pltpu.VMEM((C, 6 * C), BF16),
                pltpu.VMEM((4 * C, HID), BF16),
                pltpu.VMEM((HID, C), BF16),
                pltpu.VMEM((16, HID), BF16),
                pltpu.VMEM((16, HID), BF16),
                pltpu.VMEM((C, LANES), F32),
                pltpu.VMEM((2 * LANES, 2 * LANES), BF16),
                pltpu.VMEM((LANES, LANES), BF16),
                pltpu.VMEM((LANES, LANES), BF16),
                *[pltpu.VMEM(x.shape, x.dtype) for x in args],
                pltpu.SemaphoreType.DMA((2, 9)),
                pltpu.SemaphoreType.DMA((2, STEPS, 25)),
                pltpu.SemaphoreType.DMA((2, 9)),
                pltpu.SemaphoreType.DMA((len(args),)),
            ],
            compiler_params=pltpu.CompilerParams(
                collective_id=0, has_side_effects=True, vmem_limit_bytes=VMEM_BYTES
            ),
        )(*args)

        def hand_over(*refs):
            sems = refs[6]
            copies = [
                pltpu.make_async_copy(refs[i], refs[3 + i], sems.at[i]) for i in range(3)
            ]
            for copy in copies:
                copy.start()
            for copy in copies:
                copy.wait()

        hbm = pl.BlockSpec(memory_space=pltpu.HBM)
        results = pl.pallas_call(
            hand_over,
            out_shape=(out, out, out),
            in_specs=[hbm] * 3,
            out_specs=(hbm, hbm, hbm),
            scratch_shapes=[pltpu.SemaphoreType.DMA((3,))],
            compiler_params=pltpu.CompilerParams(vmem_limit_bytes=VMEM_BYTES),
        )(*results)
        return tuple(x.transpose(rows) for x in results)

    grid4 = P("dx", "dy", None, None)
    in_specs = (grid4, grid4, P("dx", "dy", None), grid4) + (P(),) * 8
    return jax.shard_map(
        per_device, mesh=mesh, in_specs=in_specs, out_specs=(grid4, grid4, grid4), check_vma=False
    )
```

```python
import math

import jax
import jax.numpy as jnp
from jax import lax
from jax.experimental import pallas as pl
from jax.experimental.pallas import tpu as pltpu
from jax.sharding import PartitionSpec as P

MESH = pl.DeviceIdType.MESH
F32 = jnp.float32
BF16 = jnp.bfloat16

C = 64
HID = 128
EMB = 28
NBASIS = 8
NS = 4
SLOTS = 16
STEPS = 2
CENTERS = 8
NB = 16
LANES = 128
EVALS = STEPS + 1
GB = 8
LAG = 0

VMEM_BYTES = 63 * 1024 * 1024

TIME_STEP = 0.2
CUTOFF = 4.5
SOFTEN = 0.04
MASSES = (3.0, 2.0, 1.5, 1.0)

R3 = math.sqrt(3.0)
R5 = math.sqrt(5.0)
R15 = math.sqrt(15.0)


def dot(a, b):
    return jnp.dot(a, b, preferred_element_type=F32)


def iota(shape, dim):
    return lax.broadcasted_iota(jnp.int32, shape, dim)


def column(row, size):
    square = jnp.broadcast_to(row, (size, size))
    diag = jnp.where(iota((size, size), 0) == iota((size, size), 1), square, 0.0)
    return jnp.broadcast_to(jnp.sum(diag, axis=1, keepdims=True), (size, LANES))


def lane_pick(row, index):
    return jnp.take_along_axis(
        jnp.broadcast_to(row, index.shape), index, axis=1, mode="promise_in_bounds"
    )


def gate(half):
    t = jnp.tanh(half)
    up = 1.0 + t
    act = half * up
    return act.astype(BF16), (up + act * (1.0 - t)).astype(BF16)


def kernel(
    nx, ny,
    pos_hbm, vel_hbm, kind_hbm, nbr_hbm, emb_hbm, w_in_hbm, w_two_hbm, w_val_hbm, w_env_hbm,
    w_mix_hbm, w_lat_hbm, w_out_hbm,
    pos_out, vel_out, frc_out,
    pbuf, psend, fbuf, gbuf, fsend, onehot, slotmask, zrest, zfirst, geo, back, adder, gdense, halves,
    w_in_half, w_mix_half, w_ve, w_ve_t, w_mix_t, w_two_t, w_in_t, w_hid_rows, w_out_col, same2,
    same16, seg,
    pos_ref, vel_ref, kind_ref, nbr_ref, emb_ref, w_in_ref, w_two_ref, w_val_ref, w_env_ref,
    w_mix_ref, w_lat_ref, w_out_ref,
    pos_sems, frc_sems, own_sems, load_sems,
):
    loads = [
        pltpu.make_async_copy(src, dst, load_sems.at[i])
        for i, (src, dst) in enumerate(
            (
                (pos_hbm, pos_ref), (vel_hbm, vel_ref), (kind_hbm, kind_ref), (nbr_hbm, nbr_ref),
                (emb_hbm, emb_ref), (w_in_hbm, w_in_ref), (w_two_hbm, w_two_ref),
                (w_val_hbm, w_val_ref), (w_env_hbm, w_env_ref), (w_mix_hbm, w_mix_ref),
                (w_lat_hbm, w_lat_ref), (w_out_hbm, w_out_ref),
            )
        )
    ]
    mx, my = lax.axis_index("dx"), lax.axis_index("dy")
    near = [(p, q) for p in (-1, 0, 1) for q in (-1, 0, 1) if (p, q) != (0, 0)]
    wide_area = [
        (p, q) for p in range(-2, 3) for q in range(-2, 3) if (p, q) != (0, 0)
    ]

    def device(p, q):
        return (lax.rem(mx + (p + nx), nx), lax.rem(my + (q + ny), ny))

    barrier = pltpu.get_barrier_semaphore()
    near_last = sorted(near, key=lambda o: -abs(o[0]) - abs(o[1]))
    far_first = sorted(wide_area, key=lambda o: (-abs(o[0]) - abs(o[1]), o))
    for p, q in near_last:
        pl.semaphore_signal(barrier, inc=1, device_id=device(p, q), device_id_type=MESH)

    for load in loads:
        load.start()

    def pos_copy(p, q):
        here, there = 3 * (p + 1) + q + 1, 3 * (1 - p) + 1 - q
        return pltpu.make_async_remote_copy(
            src_ref=psend, dst_ref=pbuf.at[there],
            send_sem=pos_sems.at[0, here], recv_sem=pos_sems.at[1, there],
            device_id=device(p, q), device_id_type=MESH,
        )

    def frc_copy(t, p, q):
        here, there = 5 * (p + 2) + q + 2, 5 * (2 - p) + 2 - q

        def box(ref, dp, dq):
            low_p, low_q = max(-1, p - 1), max(-1, q - 1)
            return ref.at[
                pl.ds(low_p - dp + 1, 3 - abs(p)), pl.ds(low_q - dq + 1, 3 - abs(q))
            ]

        return pltpu.make_async_remote_copy(
            src_ref=box(fsend.at[t], 0, 0), dst_ref=box(gbuf.at[t, there], p, q),
            send_sem=frc_sems.at[0, t, here], recv_sem=frc_sems.at[1, t, there],
            device_id=device(p, q), device_id_type=MESH,
        )

    def own_copy(p, q):
        here, there = 3 * (p + 1) + q + 1, 3 * (1 - p) + 1 - q
        return pltpu.make_async_remote_copy(
            src_ref=fsend.at[STEPS, p + 1, q + 1], dst_ref=fbuf.at[there],
            send_sem=own_sems.at[0, here], recv_sem=own_sems.at[1, there],
            device_id=device(p, q), device_id_type=MESH,
        )

    for load in loads[0:3]:
        load.wait()
    kinds = kind_ref[0].astype(F32)
    start = jnp.concatenate(
        [pos_ref[0, :, 0, :], kinds, vel_ref[0, :, 0, :], jnp.zeros((1, LANES), F32)], axis=0
    )
    psend[...] = start
    pl.semaphore_wait(barrier, len(near))
    for p, q in near_last:
        pos_copy(p, q).start()

    pbuf[4] = start
    fsend[...] = jnp.zeros(fsend.shape, F32)

    def inv_mass(kind):
        mass = jnp.zeros((1, LANES), F32)
        for k in range(NS):
            mass = mass + jnp.where(kind == float(k), MASSES[k], 0.0)
        return 1.0 / mass

    for load in loads[3:]:
        load.wait()
    val_t, env_t = w_val_ref[...].astype(F32), w_env_ref[...].astype(F32)
    w_ve[0 : 3 * C, :] = val_t.T.astype(BF16)
    w_ve[3 * C : 6 * C, :] = env_t.T.astype(BF16)
    w_ve_t[...] = jnp.concatenate([val_t, env_t], axis=1).astype(BF16)
    w_in_half[...] = (0.5 * w_in_ref[...].astype(F32).T).astype(BF16)
    w_mix_half[...] = (0.5 * w_mix_ref[...].astype(F32)).astype(BF16)
    w_two_t[...] = (0.5 * w_two_ref[...].astype(F32).T).astype(BF16)
    w_in_t[...] = w_in_ref[0:16]
    out_col = column(w_out_ref[...].reshape(1, C), C)
    w_out_col[...] = out_col
    w_hid = jnp.sum(w_lat_ref[...].astype(F32) * out_col, axis=0, keepdims=True)
    w_hid_col = column(w_hid, HID)
    w_mix_t[...] = (
        (0.5 * w_mix_ref[...].astype(F32)) * jnp.concatenate([w_hid_col] * 2, axis=1)
    ).T.astype(BF16)
    hid_hi = w_hid.astype(BF16).astype(F32)
    row16 = iota((16, LANES), 0)
    w_hid_rows[...] = jnp.where(
        row16 == 0, hid_hi, jnp.where(row16 == 1, w_hid - hid_hi, 0.0)
    ).astype(BF16)
    lane_r, lane_c = iota((LANES, LANES), 0), iota((LANES, LANES), 1)
    together = jnp.where(lane_r // SLOTS == lane_c // SLOTS, 1.0 / SLOTS, 0.0)
    same16[...] = together.astype(BF16)
    pair_r, pair_c = iota((2 * LANES, 2 * LANES), 0), iota((2 * LANES, 2 * LANES), 1)
    same2[...] = jnp.where(pair_r // SLOTS == pair_c // SLOTS, 1.0 / SLOTS, 0.0).astype(BF16)
    adder[...] = jnp.where(
        iota((16, C), 0) == iota((16, C), 1) // 8, 1.0 / SLOTS, 0.0
    ).astype(BF16)
    seg[...] = jnp.where(lane_r // SLOTS == lane_c % CENTERS, 1.0, 0.0).astype(BF16)

    nbrs = nbr_ref[0, 0]
    valid = jnp.where(nbrs >= 0, 1.0, 0.0)
    index = jnp.maximum(nbrs, 0)
    atom = jnp.bitwise_and(index, LANES - 1)
    slot = jnp.right_shift(index, 7)
    gdense[0] = atom.astype(F32)
    gdense[1] = slot.astype(F32)
    row_b, lane_b = iota((NB, LANES), 0), iota((NB, LANES), 1)
    centre_index = row_b * CENTERS + lane_b // SLOTS
    owner = jnp.where(lane_b // CENTERS == row_b, 1.0, 0.0)
    slot_x = (slot // 3).astype(F32) - 1.0
    slot_y = jnp.remainder(slot, 3).astype(F32) - 1.0

    def one_hots(i, carry):
        for j in range(2):
            b = 2 * i + j
            onehot[i, :, j * LANES : (j + 1) * LANES] = jnp.where(
                lane_r.astype(F32) == gdense[0, pl.ds(b, 1), :], 1.0, 0.0
            ).astype(BF16)
            slotmask[b] = jnp.where(row16.astype(F32) == gdense[1, pl.ds(b, 1), :], 1.0, 0.0)
        return carry

    lax.fori_loop(0, NB // 2, one_hots, 0)

    row8 = iota((8, LANES), 0)
    emb_t = emb_ref[...].astype(F32).T
    blank = jnp.zeros((EMB, NS), F32)
    emb_both = jnp.concatenate(
        [jnp.concatenate([emb_t, blank], axis=1), jnp.concatenate([blank, emb_t], axis=1)], axis=0
    ).astype(BF16)

    for p, q in near:
        pos_copy(p, q).wait_recv()
    far_kind = jnp.zeros((NB, LANES), F32)
    for o in range(9):
        far_kind = jnp.where(slot == o, lane_pick(pbuf[o, 3:4, :], atom), far_kind)
    for o in range(9):
        halves[o] = jnp.broadcast_to(
            (0.5 * TIME_STEP) * inv_mass(pbuf[o, 3:4, :]), (8, LANES)
        )
    gdense[0] = lane_pick(kinds, centre_index)
    gdense[1] = far_kind
    kind_of = jnp.where(row8 < NS, row8, row8 - NS).astype(F32)
    chosen = jnp.concatenate(
        [
            jnp.where(
                kind_of == jnp.where(row8 < NS, gdense[0, b : b + 1, :], gdense[1, b : b + 1, :]),
                1.0, 0.0,
            ).astype(BF16)
            for b in range(NB)
        ],
        axis=1,
    )
    looked = dot(emb_both, chosen)
    for b in range(NB):
        zfirst[b] = looked[0:8, b * LANES : (b + 1) * LANES]
        zrest[b] = looked[8 : 2 * EMB, b * LANES : (b + 1) * LANES].astype(BF16)

    slot_lane = lane_b // SLOTS * SLOTS + row_b
    lane_atom = lane_b // SLOTS

    def wide(parts):
        return jnp.concatenate(parts, axis=1)

    def tall(parts):
        return jnp.concatenate(parts, axis=0)

    def part(x, j):
        return x[:, j * LANES : (j + 1) * LANES]

    def order(x, l):
        return x[l * C : (l + 1) * C]

    def corner(a, b):
        zero = jnp.zeros((LANES, LANES), BF16)
        return tall([wide([a, zero]), wide([zero, b])])

    def chain(tiles):
        count = len(tiles)
        each = range(count)

        def gather(values):
            return [[] for _ in range(values)]

        def mix_slots(x, gram):
            first = dot(tall([order(x[i], 0) for i in each]), same2[...]).astype(BF16)
            yield None
            mixed = []
            for i in each:
                mixed.append(
                    tall(
                        [order(first, i)]
                        + [dot(order(x[i], l), gram[i][l - 1]).astype(BF16) for l in (1, 2)]
                    )
                )
                yield None
            yield mixed

        cut, cut16, a1, hidden, slope1, pre, latent16, value, envw, a2, hidden2, slope2 = gather(12)
        d_a2, readout, d_mixed, d_value, d_envat, d_latent, d_hidden, picks, gram = gather(9)
        for i in each:
            pair = (2 * tiles[i], 2 * tiles[i] + 1)
            cut.append(wide([geo[b, 16:17, :] for b in pair]))
            cut16.append(cut[i].astype(BF16))
            top = wide([tall([geo[b, 0:8, :], zfirst[b]]) for b in pair])
            zin = tall([top.astype(BF16), wide([zrest[b] for b in pair])])
            a1.append(dot(w_in_half[...], zin))
            yield
        for i in each:
            act, slope = gate(a1[i])
            hidden.append(act)
            slope1.append(slope)
            yield
        for i in each:
            pre.append(dot(w_two_ref[...], hidden[i]))
            latent16.append((pre[i] * cut[i]).astype(BF16))
            yield
        for i in each:
            blockwise = []
            for b in (2 * tiles[i], 2 * tiles[i] + 1):
                sph = geo[b, 8:16, :]
                rows = [sph[m : m + 1] for m in range(8)]
                far = [lane_pick(row, slot_lane) for row in rows]
                terms = [far[m] * rows[m] for m in range(8)]
                compact = [
                    (terms[0] + terms[1]) + terms[2],
                    ((terms[3] + terms[4]) + (terms[5] + terms[6])) + terms[7],
                ]
                picks.append(far)
                blockwise.append([tall([x.astype(BF16)] * CENTERS) * same16[...] for x in compact])
            gram.append([corner(blockwise[0][l], blockwise[1][l]) for l in range(2)])
            yield
        for i in each:
            value_envw = dot(w_ve[...], latent16[i])
            value.append(value_envw[0 : 3 * C].astype(BF16))
            envw.append(value_envw[3 * C : 6 * C].astype(BF16))
            yield
        for env_at in mix_slots(envw, gram):
            if env_at is None:
                yield
        for i in each:
            mixed = tall([latent16[i], value[i] * env_at[i]])
            a2.append(dot(w_mix_half[...], mixed))
            yield
        for i in each:
            act, slope = gate(a2[i])
            hidden2.append(act)
            d_a2.append(slope * cut16[i])
            yield
        for i in each:
            d_mixed.append(dot(w_mix_t[...], d_a2[i]))
            d_scal = d_mixed[i][C : 4 * C].astype(BF16)
            d_value.append(d_scal * env_at[i])
            d_envat.append(d_scal * value[i])
            yield
        for d_envw in mix_slots(d_envat, gram):
            if d_envw is None:
                yield
        for i in each:
            both = dot(w_hid_rows[...], hidden2[i])
            readout.append(both[0:1] + both[1:2])
            energy_part = wide([w_out_col[...]] * 2) * cut[i]
            rest = dot(w_ve_t[...], tall([d_value[i], d_envw[i]]))
            d_latent.append((d_mixed[i][0:C] + rest) + energy_part)
            d_cut = readout[i] + jnp.sum(
                pre[i] * (d_latent[i] + energy_part), axis=0, keepdims=True
            )
            for j in range(2):
                back[2 * tiles[i] + j, 16:17, :] = part(d_cut, j)
            yield
        for i in each:
            d_hidden.append(dot(w_two_t[...], (d_latent[i] * cut[i]).astype(BF16)).astype(BF16))
            yield
        stacks = []
        for i in each:
            for j in range(2):
                dq, ew = part(d_envat[i], j), part(envw[i], j)
                left = tall([order(dq, 1), order(ew, 1), order(dq, 2), order(ew, 2)])
                right = corner(
                    tall([order(ew, 1), order(dq, 1)]), tall([order(ew, 2), order(dq, 2)])
                )
                pair = lax.dot_general(
                    left, right, (((0,), (0,)), ((), ())), preferred_element_type=F32
                )
                sums = []
                for l in range(2):
                    full = part(pair, l)
                    own = full[0:SLOTS]
                    for a in range(1, CENTERS):
                        own = jnp.where(
                            lane_atom == a, full[a * SLOTS : (a + 1) * SLOTS], own
                        )
                    sums.append(own)
                stack = []
                for m in range(8):
                    product = sums[0 if m < 3 else 1] * picks[2 * i + j][m]
                    stack.append(product[0:8] + product[8:16])
                stacks.append(tall(stack).astype(BF16))
                yield
        for i in each:
            d_basis = dot(w_in_t[...], d_hidden[i] * slope1[i])
            for j in range(2):
                back[2 * tiles[i] + j, 0:8, :] = part(d_basis, j)[0:8]
            yield
        for i in each:
            d_sph = dot(adder[...], wide(stacks[2 * i : 2 * i + 2]))
            for j in range(2):
                back[2 * tiles[i] + j, 8:16, :] = part(d_sph, j)[0:8]
            yield

    def run_chains(lag):
        waiting = [chain(list(range(i, i + GB // 2))) for i in range(0, NB // 2, GB // 2)]
        running = []
        step = 0
        while waiting or running:
            while waiting and (lag == 0 or step % lag == 0):
                running.append(waiting.pop(0))
                if lag:
                    break
            for one in list(running):
                if next(one, 0) == 0:
                    running.remove(one)
            step += 1

    middle = iota((3, LANES), 0) == 1

    def evaluate(t, carry):
        here = pbuf[4]
        rel = []
        for k in range(3):
            far = jnp.zeros((NB, LANES), F32)
            for o in range(9):
                far = jnp.where(slot == o, lane_pick(pbuf[o, k : k + 1, :], atom), far)
            if k == 0:
                far = far + slot_x
            if k == 1:
                far = far + slot_y
            rel.append(far - lane_pick(here[k : k + 1], centre_index))
        dist_sq = rel[0] * rel[0] + rel[1] * rel[1] + rel[2] * rel[2] + SOFTEN
        dist = jnp.sqrt(dist_sq)
        inv = 1.0 / dist
        ux, uy, uz = rel[0] * inv, rel[1] * inv, rel[2] * inv
        fall = 1.0 - dist_sq * (1.0 / (CUTOFF * CUTOFF))
        cut = valid * fall * fall
        theta = dist * (math.pi / CUTOFF)
        sin1, cos1 = jnp.sin(theta), jnp.cos(theta)
        sines, cosines = [sin1], [cos1]
        for n in range(1, NBASIS):
            s, c = sines[-1], cosines[-1]
            sines.append(s * cos1 + c * sin1)
            cosines.append(c * cos1 - s * sin1)
        for n in range(NBASIS):
            geo[:, n, :] = sines[n] * inv * cut
        sph = (
            R3 * ux, R3 * uy, R3 * uz, R15 * ux * uy, R15 * uy * uz,
            0.5 * R5 * (3.0 * uz * uz - 1.0), R15 * ux * uz, 0.5 * R15 * (ux * ux - uy * uy),
        )
        for m in range(8):
            geo[:, 8 + m, :] = sph[m]
        geo[:, 16, :] = cut

        run_chains(LAG)

        d1, d2, d3, d4, d5, d6, d7, d8 = [back[:, 8 + m, :] for m in range(8)]
        du = (
            R3 * d1 + R15 * (uy * d4 + uz * d7 + ux * d8),
            R3 * d2 + R15 * (ux * d4 + uz * d5 - uy * d8),
            R3 * d3 + R15 * (uy * d5 + ux * d7) + (3.0 * R5) * (uz * d6),
        )
        by_sin = jnp.zeros((NB, LANES), F32)
        by_cos = jnp.zeros((NB, LANES), F32)
        for n in range(NBASIS):
            d_basis = back[:, n, :]
            by_sin = by_sin + d_basis * sines[n]
            by_cos = by_cos + (d_basis * cosines[n]) * ((n + 1) * math.pi / CUTOFF)
        by_sin = by_sin * inv
        d_cut = back[:, 16, :] + by_sin
        d_dist = cut * inv * (by_cos - by_sin) - inv * (du[0] * ux + du[1] * uy + du[2] * uz)
        d_sq = 0.5 * inv * d_dist - d_cut * (valid * fall) * (2.0 / (CUTOFF * CUTOFF))
        grads = [(du[k] * inv + 2.0 * rel[k] * d_sq) * valid for k in range(3)]

        split = []
        for k in range(3):
            high = grads[k].astype(BF16).astype(F32)
            gdense[k] = high
            gdense[3 + k] = grads[k] - high
        segs = dot(gdense[...].reshape(6 * NB, LANES).astype(BF16), seg[...])
        centre = [
            jnp.sum(
                (segs[k * NB : (k + 1) * NB] + segs[(3 + k) * NB : (4 + k) * NB]) * owner,
                axis=0, keepdims=True,
            )
            for k in range(3)
        ]
        sums = [jnp.zeros((6 * 16, LANES), F32)] * 2
        for i in range(NB // 2):
            left = wide(
                [
                    tall([gdense[k, b : b + 1, :] * slotmask[b] for k in range(6)]).astype(BF16)
                    for b in (2 * i, 2 * i + 1)
                ]
            )
            sums[i % 2] = sums[i % 2] + lax.dot_general(
                left, onehot[i], (((1,), (1,)), ((), ())), preferred_element_type=F32
            )
        scattered = sums[0] + sums[1]
        ghost = [
            scattered[k * 16 : (k + 1) * 16] + scattered[(3 + k) * 16 : (4 + k) * 16]
            for k in range(3)
        ]
        for k in range(3):
            for p in range(3):
                terms = -ghost[k][3 * p : 3 * p + 3]
                if p == 1:
                    terms = terms + jnp.where(middle, centre[k], 0.0)
                fsend[t, p, :, k, :] = terms

        @pl.when(t < STEPS)
        def _():
            for p, q in far_first:
                frc_copy(t, p, q).start()
            for p, q in reversed(far_first):
                frc_copy(t, p, q).wait_recv()
            for dp in range(-1, 2):
                for dq in range(-1, 2):
                    force = fsend[t, dp + 1, dq + 1]
                    for a in range(dp - 1, dp + 2):
                        for b in range(dq - 1, dq + 2):
                            if (a, b) != (0, 0):
                                force = force + gbuf[t, 5 * (a + 2) + b + 2, dp + 1, dq + 1]
                    slot_at = 3 * (dp + 1) + dq + 1
                    kick = halves[slot_at, 0:1, :] * force[0:3]
                    speed = pbuf[slot_at, 4:7, :]
                    speed = speed + jnp.where(t > 0, 1.0, 0.0) * kick
                    speed = speed + kick
                    pbuf[slot_at, 4:7, :] = speed
                    pbuf[slot_at, 0:3, :] = pbuf[slot_at, 0:3, :] + TIME_STEP * speed
            for p, q in far_first:
                frc_copy(t, p, q).wait_send()

        return carry

    lax.fori_loop(0, EVALS, evaluate, 0)
    for p, q in near:
        own_copy(p, q).start()
    for p, q in near:
        pos_copy(p, q).wait_send()
    for p, q in near:
        own_copy(p, q).wait_recv()
    force = fsend[STEPS, 1, 1]
    for p, q in near:
        force = force + fbuf[3 * (p + 1) + q + 1]
    speed = pbuf[4, 4:7, :] + halves[4, 0:1, :] * force[0:3]
    pos_out[0, :, 0, :] = pbuf[4, 0:3, :]
    vel_out[0, :, 0, :] = speed
    frc_out[0, :, 0, :] = force[0:3]
    for p, q in near:
        own_copy(p, q).wait_send()


def solution(mesh):
    nx, ny = mesh.shape["dx"], mesh.shape["dy"]

    def per_device(positions, velocities, species, neighbours, emb, w_in, w_two, w_val, w_env, *more):
        rows = (0, 2, 1, 3)
        args = (
            positions.transpose(rows), velocities.transpose(rows), species, neighbours, emb,
            w_in.T, w_two, w_val.T, w_env.T, *more,
        )

        def body(*refs):
            kernel(nx, ny, *refs)

        vmem = pl.BlockSpec(memory_space=pltpu.VMEM)
        out = jax.ShapeDtypeStruct((1, 3, 1, LANES), F32)
        results = pl.pallas_call(
            body,
            out_shape=(out, out, out),
            in_specs=[pl.BlockSpec(memory_space=pltpu.HBM)] * len(args),
            out_specs=(vmem, vmem, vmem),
            scratch_shapes=[
                pltpu.VMEM((9, 8, LANES), F32),
                pltpu.VMEM((8, LANES), F32),
                pltpu.VMEM((9, 4, LANES), F32),
                pltpu.VMEM((STEPS, 25, 3, 3, 4, LANES), F32),
                pltpu.VMEM((EVALS, 3, 3, 4, LANES), F32),
                pltpu.VMEM((NB // 2, LANES, 2 * LANES), BF16),
                pltpu.VMEM((NB, 16, LANES), F32),
                pltpu.VMEM((NB, 48, LANES), BF16),
                pltpu.VMEM((NB, 8, LANES), F32),
                pltpu.VMEM((NB, 24, LANES), F32),
                pltpu.VMEM((NB, 24, LANES), F32),
                pltpu.VMEM((16, C), BF16),
                pltpu.VMEM((6, NB, LANES), F32),
                pltpu.VMEM((9, 8, LANES), F32),
                pltpu.VMEM((HID, NBASIS + 2 * EMB), BF16),
                pltpu.VMEM((HID, 4 * C), BF16),
                pltpu.VMEM((6 * C, C), BF16),
                pltpu.VMEM((C, 6 * C), BF16),
                pltpu.VMEM((4 * C, HID), BF16),
                pltpu.VMEM((HID, C), BF16),
                pltpu.VMEM((16, HID), BF16),
                pltpu.VMEM((16, HID), BF16),
                pltpu.VMEM((C, LANES), F32),
                pltpu.VMEM((2 * LANES, 2 * LANES), BF16),
                pltpu.VMEM((LANES, LANES), BF16),
                pltpu.VMEM((LANES, LANES), BF16),
                *[pltpu.VMEM(x.shape, x.dtype) for x in args],
                pltpu.SemaphoreType.DMA((2, 9)),
                pltpu.SemaphoreType.DMA((2, STEPS, 25)),
                pltpu.SemaphoreType.DMA((2, 9)),
                pltpu.SemaphoreType.DMA((len(args),)),
            ],
            compiler_params=pltpu.CompilerParams(
                collective_id=0, has_side_effects=True, vmem_limit_bytes=VMEM_BYTES
            ),
        )(*args)

        def hand_over(*refs):
            sems = refs[6]
            copies = [
                pltpu.make_async_copy(refs[i], refs[3 + i], sems.at[i]) for i in range(3)
            ]
            for copy in copies:
                copy.start()
            for copy in copies:
                copy.wait()

        hbm = pl.BlockSpec(memory_space=pltpu.HBM)
        results = pl.pallas_call(
            hand_over,
            out_shape=(out, out, out),
            in_specs=[hbm] * 3,
            out_specs=(hbm, hbm, hbm),
            scratch_shapes=[pltpu.SemaphoreType.DMA((3,))],
            compiler_params=pltpu.CompilerParams(vmem_limit_bytes=VMEM_BYTES),
        )(*results)
        return tuple(x.transpose(rows) for x in results)

    grid4 = P("dx", "dy", None, None)
    in_specs = (grid4, grid4, P("dx", "dy", None), grid4) + (P(),) * 8
    return jax.shard_map(
        per_device, mesh=mesh, in_specs=in_specs, out_specs=(grid4, grid4, grid4), check_vma=False
    )
```
